32 devices in a mesh: tok: 8 (over z, y), out: 4 (over x, core).
Axes of the slice: x: 2, y: 2, z: 4, core: 2. Of those that a mesh axis runs over, the one named last changes fastest.
Arguments:
- acts: bfloat16 [3, 512, 8192], P(None, 'tok'), may hold values from -6 to 6
- grads: bfloat16 [3, 512, 4096], P(None, 'tok', 'out'), may hold values from -6 to 6
- act_basis: float32 [1024, 8, 8], P('tok'), may hold values from -2 to 2
- grad_basis: float32 [512, 8, 8], P('out'), may hold values from -2 to 2
Outputs:
- eigen_corr: float32 [4096, 8192], P('out', 'tok')
The draws below stay inside these ranges and needn't reach their ends.
All inputs are finite; a program needn't handle non-finite values.
Results may differ from the reference program's by a relative error of at most 0.014.
Values may be sent and summed in bfloat16 or wider, within the bound.
No kernel may reach another device: no remote copies, remote signals or barrier semaphores. Data moves between devices by JAX's collectives and lax.ppermute only.
A program may use at most 128 MiB of HBM per device.

```python
import jax
import jax.numpy as jnp
from jax import lax

DIN = 8192
DOUT = 4096
SEQS = 3
SEQ_LEN = 512


def levels(key, dims, pieces, low, top_value):
    level = 1.0
    for dim, parts in pieces:
        heights = jax.random.uniform(jax.random.fold_in(jax.random.fold_in(key, 6), dim), (parts,), jnp.float32, low / len(pieces), top_value / len(pieces))
        level = level * jnp.repeat(jnp.exp(heights), dims[dim] // parts).reshape((-1,) + (1,) * (len(dims) - 1 - dim))
    return level


def scatter_about(key, extent, spread, limit, pieces=(), kind=jnp.bfloat16):
    gain = levels(key, extent, pieces, -0.22, 0.18) if pieces else 1.0
    result = jax.random.normal(key, extent, jnp.float32) * spread * gain
    return jnp.minimum(jnp.maximum(result, -limit), limit).astype(kind)


def setup_inputs(seed: int = 0) -> dict:
    seeds = jax.random.split(jax.random.key(seed), 5)
    return {
        "acts": scatter_about(seeds[0], (SEQS, SEQ_LEN, DIN), 1.0, 6.0, ((1, 8),)),
        "grads": scatter_about(seeds[1], (SEQS, SEQ_LEN, DOUT), 1.0, 6.0, ((1, 8), (2, 4))),
        "act_basis": scatter_about(seeds[2], (DIN // 8, 8, 8), 8 ** -0.5, 2.0, ((0, 8),), jnp.float32),
        "grad_basis": scatter_about(seeds[3], (DOUT // 8, 8, 8), 8 ** -0.5, 2.0, ((0, 4),), jnp.float32),
    }


def rotate(values, basis):
    seqs, rows, width = values.shape
    split = values.astype(jnp.float32).reshape(seqs, rows, width // 8, 8)
    turned = jnp.einsum("stbp,bpq->stbq", split, basis.astype(jnp.float32), precision=lax.Precision.HIGHEST)
    return turned.reshape(seqs, rows, width).astype(jnp.bfloat16)


def reference(acts, grads, act_basis, grad_basis):
    rot_acts = rotate(acts, act_basis)
    rot_grads = rotate(grads, grad_basis)
    scale = SEQ_LEN ** -0.5

    def accumulate(total, pair):
        grad_seq, act_seq = pair
        corr = jnp.dot(grad_seq.T, act_seq, preferred_element_type=jnp.float32) * scale
        return total + corr * corr, None

    start_total = jnp.zeros((DOUT, DIN), jnp.float32)
    eigen_corr, unused = lax.scan(accumulate, start_total, (rot_grads, rot_acts))
    return eigen_corr
```

```python
import functools

import jax
import jax.numpy as jnp
from jax import lax
from jax.experimental import pallas as pl
from jax.experimental.pallas import tpu as pltpu
from jax.sharding import PartitionSpec as P

BF, F32 = jnp.bfloat16, jnp.float32


def dot(a, b, contract):
    return lax.dot_general(a, b, (contract, ((), ())), preferred_element_type=F32)


def split(value):
    high = value.astype(BF)
    return high, (value - high.astype(F32)).astype(BF)


def spread_kernel(transposed, basis_ref, high_ref, low_ref):
    groups, span, _ = high_ref.shape
    blocks = basis_ref.shape[1]
    parts = split(basis_ref[...])
    iota = lambda shape, dim: lax.broadcasted_iota(jnp.int32, shape, dim)
    pq_row, pq_col = (
        (iota((span, 64), 1) % 8, iota((64, span), 0) // 8)
        if transposed
        else (iota((span, 64), 1) // 8, iota((64, span), 0) % 8)
    )
    keep = pq_row == iota((span, 64), 0) % 8
    repeat = (pq_col == iota((64, span), 1) % 8).astype(BF)
    diagonal = iota((span, span), 0) // 8 == iota((span, span), 1) // 8
    for g in range(groups):
        pick = iota((span, blocks), 0) // 8 + g * (span // 8) == iota((span, blocks), 1)
        pick = pick.astype(BF)
        for part, out_ref in zip(parts, (high_ref, low_ref)):
            rows = dot(pick, part, ((1,), (1,)))
            rows = jnp.where(keep, rows, 0.0).astype(BF)
            full = dot(rows, repeat, ((1,), (0,)))
            out_ref[g] = jnp.where(diagonal, full, 0.0).astype(BF)


def spread(basis, transposed):
    blocks = basis.shape[0]
    span = min(256, blocks * 8)
    groups = blocks * 8 // span
    flat = jnp.transpose(basis, (1, 2, 0)).reshape(64, blocks)
    shape = jax.ShapeDtypeStruct((groups, span, span), BF)
    return pl.pallas_call(
        functools.partial(spread_kernel, transposed), out_shape=(shape, shape)
    )(flat)


def main_kernel(n, m, scale, place_ref, *refs):
    n_acts = n // 2 * m
    acts = refs[:n_acts]
    grads = refs[n_acts : n_acts + n]
    wa_high, wa_low, wg_high, wg_low, out_ref, a_raw, g_raw, a_rot, sems = refs[n_acts + n :]
    seqs, length, width = a_raw.shape
    quarter = length // (n * m)
    rows = length // n
    span = wa_high.shape[1]
    tile = out_ref.shape[0]

    def copies():
        index = 0
        for k in range(n // 2):
            for j in range(m):
                for y in range(2):
                    start = (2 * k + y) * rows + (place_ref[0] ^ j) * quarter
                    yield pltpu.make_async_copy(
                        acts[k * m + j].at[y],
                        a_raw.at[:, pl.ds(pl.multiple_of(start, quarter), quarter), :],
                        sems.at[index],
                    )
                    index += 1
        for k in range(n):
            yield pltpu.make_async_copy(
                grads[k], g_raw.at[:, pl.ds(k * rows, rows), :], sems.at[index]
            )
            index += 1

    @pl.when(pl.program_id(0) == 0)
    def _():
        for copy in copies():
            copy.start()
        for copy in copies():
            copy.wait()
        for s in range(seqs):
            for g in range(width // span):
                columns = pl.ds(g * span, span)
                block = a_raw[s, :, columns]
                turned = dot(block, wa_high[g], ((1,), (0,))) + dot(block, wa_low[g], ((1,), (0,)))
                a_rot[s, :, columns] = turned.astype(BF)

    step = pl.program_id(0)
    columns = pl.ds(pl.multiple_of(step * tile, tile), tile)
    total = None
    for s in range(seqs):
        block = g_raw[s, :, columns]
        turned = dot(wg_high[step], block, ((1,), (1,))) + dot(wg_low[step], block, ((1,), (1,)))
        corr = dot(turned.astype(BF), a_rot[s], ((1,), (0,))) * scale
        total = corr * corr if total is None else total + corr * corr
    out_ref[...] = total


def multiply(n, m, place, acts, grads, wa, wg):
    rows, outs = grads[0].shape[1:]
    seqs, width = acts[0].shape[1], acts[0].shape[-1]
    length = rows * n
    tile = wg[0].shape[1]
    anywhere = pl.BlockSpec(memory_space=pl.ANY)
    vmem = pl.BlockSpec(memory_space=pltpu.VMEM)
    return pl.pallas_call(
        functools.partial(main_kernel, n, m, length ** (-0.5)),
        grid=(outs // tile,),
        in_specs=[pl.BlockSpec(memory_space=pltpu.SMEM)]
        + [anywhere] * (len(acts) + len(grads))
        + [vmem] * 4,
        out_specs=pl.BlockSpec((tile, width), lambda i: (i, 0)),
        out_shape=jax.ShapeDtypeStruct((outs, width), F32),
        scratch_shapes=[
            pltpu.VMEM((seqs, length, width), BF),
            pltpu.VMEM((seqs, length, outs), BF),
            pltpu.VMEM((seqs, length, width), BF),
            pltpu.SemaphoreType.DMA((2 * len(acts) + len(grads),)),
        ],
        compiler_params=pltpu.CompilerParams(vmem_limit_bytes=48 * 2**20),
    )(place, *acts, *grads, *wa, *wg)


def shards(acts, grads, act_basis, grad_basis):
    n, m = lax.axis_size("tok"), lax.axis_size("out")
    half = n // 2
    t, q = lax.axis_index("tok"), lax.axis_index("out")
    z, y = t // 2, t % 2
    seqs, rows, total = acts.shape
    width, quarter = total // n, rows // m

    def over_y(value):
        return lax.ppermute(value, "tok", [(i, i ^ 1) for i in range(n)])

    def over_z(value, shift):
        return lax.ppermute(
            value, "tok", [(i, (i // 2 + shift) % half * 2 + i % 2) for i in range(n)]
        )

    def over_out(value, bit):
        return lax.ppermute(value, "out", [(i, i ^ bit) for i in range(m)])

    wa = spread(act_basis, False)
    wg = spread(grad_basis, True)

    part = lax.dynamic_slice_in_dim(acts, q * quarter, quarter, 1)
    part = part.reshape(seqs, quarter, half, 2, width).transpose(3, 2, 0, 1, 4)
    mine = lax.dynamic_index_in_dim(part, y, 0)
    other = over_y(lax.dynamic_index_in_dim(part, 1 - y, 0))
    both = jnp.concatenate([mine, other], 0)

    ring = {0: grads}
    for k in range(1, half // 2 + 1):
        ring[k] = over_z(ring[k - 1], 1)
    for k in range(1, (half - 1) // 2 + 1):
        ring[half - k] = over_z(ring[(half - k + 1) % half], -1)
    all_grads = []
    for k in range(half):
        all_grads += [ring[k], over_y(ring[k])]

    all_acts = []
    for k in range(half):
        sent = lax.dynamic_index_in_dim(both, (z + k) % half, 1, keepdims=False)
        have = [sent if k == 0 else over_z(sent, k)]
        bit = m // 2
        held = {0: have[0]}
        while bit:
            held.update({j | bit: over_out(value, bit) for j, value in list(held.items())})
            bit //= 2
        all_acts += [held[j] for j in range(m)]

    place = q.astype(jnp.int32).reshape(1)
    return multiply(n, m, place, all_acts, all_grads, wa, wg)


def solution(mesh):
    placed = (
        P(None, "tok", None),
        P(None, "tok", "out"),
        P("tok", None, None),
        P("out", None, None),
    )
    return jax.shard_map(
        shards, mesh=mesh, in_specs=placed, out_specs=P("out", "tok"), check_vma=False
    )
```

```python
import functools

import jax
import jax.numpy as jnp
from jax import lax
from jax.experimental import pallas as pl
from jax.experimental.pallas import tpu as pltpu
from jax.sharding import PartitionSpec as P

BF, F32 = jnp.bfloat16, jnp.float32
SCALARS = pl.BlockSpec(memory_space=pltpu.SMEM)
VECTORS = pl.BlockSpec(memory_space=pltpu.VMEM)


def dot(a, b, contract):
    return lax.dot_general(a, b, (contract, ((), ())), preferred_element_type=F32)


def split(value):
    high = value.astype(BF)
    return high, (value - high.astype(F32)).astype(BF)


def run_all(copies):
    for copy in copies:
        copy.start()
    for copy in copies:
        copy.wait()


def limit(*specs):
    total = sum(2 * s.size * jnp.dtype(s.dtype).itemsize for s in specs)
    return total + 8 * 2**20


def spread_one(transposed, basis_ref, high_ref, low_ref):
    groups, span, _ = high_ref.shape
    blocks = basis_ref.shape[1]
    parts = split(basis_ref[...])
    iota = lambda shape, dim: lax.broadcasted_iota(jnp.int32, shape, dim)
    pq_row, pq_col = (
        (iota((span, 64), 1) % 8, iota((64, span), 0) // 8)
        if transposed
        else (iota((span, 64), 1) // 8, iota((64, span), 0) % 8)
    )
    keep = pq_row == iota((span, 64), 0) % 8
    repeat = (pq_col == iota((64, span), 1) % 8).astype(BF)
    diagonal = iota((span, span), 0) // 8 == iota((span, span), 1) // 8
    for g in range(groups):
        pick = iota((span, blocks), 0) // 8 + g * (span // 8) == iota((span, blocks), 1)
        pick = pick.astype(BF)
        for part, out_ref in zip(parts, (high_ref, low_ref)):
            rows = dot(pick, part, ((1,), (1,)))
            rows = jnp.where(keep, rows, 0.0).astype(BF)
            full = dot(rows, repeat, ((1,), (0,)))
            out_ref[g] = jnp.where(diagonal, full, 0.0).astype(BF)


def spread_kernel(a_ref, g_ref, a_high, a_low, g_high, g_low):
    spread_one(False, a_ref, a_high, a_low)
    spread_one(True, g_ref, g_high, g_low)


def spread(act_basis, grad_basis):
    flat, shapes = [], []
    for basis in (act_basis, grad_basis):
        blocks = basis.shape[0]
        span = min(256, blocks * 8)
        flat.append(jnp.transpose(basis, (1, 2, 0)).reshape(64, blocks))
        shapes += [jax.ShapeDtypeStruct((blocks * 8 // span, span, span), BF)] * 2
    out = pl.pallas_call(
        spread_kernel,
        out_shape=tuple(shapes),
        compiler_params=pltpu.CompilerParams(vmem_limit_bytes=limit(*shapes)),
        name="spread",
    )(*flat)
    return out[:2], out[2:]


def cut_kernel(half, where_ref, acts_ref, *refs):
    *outs, sems = refs
    q, z, y = where_ref[0], where_ref[1], where_ref[2]
    _, _, quarter, width = outs[0].shape[0:4]
    copies = []
    for k in range(half):
        for other in range(2):
            column = ((z + k) % half * 2 + (y ^ other)) * width
            copies.append(
                pltpu.make_async_copy(
                    acts_ref.at[
                        :,
                        pl.ds(pl.multiple_of(q * quarter, quarter), quarter),
                        pl.ds(pl.multiple_of(column, width), width),
                    ],
                    outs[k].at[other],
                    sems.at[2 * k + other],
                )
            )
    run_all(copies)


def cut(acts, where, n, m):
    seqs, rows, total = acts.shape
    shape = jax.ShapeDtypeStruct((2, seqs, rows // m, total // n), BF)
    return pl.pallas_call(
        functools.partial(cut_kernel, n // 2),
        in_specs=[SCALARS, pl.BlockSpec(memory_space=pltpu.HBM)],
        out_specs=[VECTORS] * (n // 2),
        out_shape=[shape] * (n // 2),
        scratch_shapes=[pltpu.SemaphoreType.DMA((n,))],
        compiler_params=pltpu.CompilerParams(vmem_limit_bytes=limit(*[shape] * (n // 2))),
        name="cut",
    )(where, acts)


def part_kernel(*refs):
    *pieces, stay, go = refs
    for k, piece in enumerate(pieces):
        stay[k], go[k] = piece[0], piece[1]


def part(pieces):
    half = len(pieces)
    shape = jax.ShapeDtypeStruct((half, *pieces[0].shape[1:]), BF)
    return pl.pallas_call(
        part_kernel,
        in_specs=[VECTORS] * half,
        out_specs=[VECTORS] * 2,
        out_shape=[shape] * 2,
        compiler_params=pltpu.CompilerParams(vmem_limit_bytes=limit(shape, shape)),
        name="part",
    )(*pieces)


def turn_acts_kernel(order, m, where_ref, *refs):
    pieces, (high, low, out_ref) = refs[: 2 * m], refs[2 * m :]
    half, seqs, quarter, width = pieces[0].shape
    rows = quarter * m
    groups, span, _ = high.shape
    for j in range(m):
        place = pl.multiple_of((where_ref[0] ^ j) * quarter, quarter)
        for other in range(2):
            piece = pieces[2 * j + other]
            for g in range(groups):
                columns = pl.ds(g * span, span)
                block = piece[:, :, :, columns].reshape(half * seqs * quarter, span)
                turned = dot(block, high[g], ((1,), (0,))) + dot(block, low[g], ((1,), (0,)))
                turned = turned.astype(BF).reshape(half, seqs, quarter, span)
                for at, k in enumerate(order):
                    to = pl.ds(place + (2 * at + other) * rows, quarter)
                    out_ref[:, to, columns] = turned[k]


def turn_acts(where, pieces, parts, order, m):
    half, seqs, quarter, width = pieces[0].shape
    shape = jax.ShapeDtypeStruct((seqs, 2 * half * m * quarter, width), BF)
    return pl.pallas_call(
        functools.partial(turn_acts_kernel, order, m),
        in_specs=[SCALARS] + [VECTORS] * (2 * m + 2),
        out_specs=VECTORS,
        out_shape=shape,
        compiler_params=pltpu.CompilerParams(vmem_limit_bytes=limit(shape, shape)),
        name="turn_acts",
    )(where, *pieces, *parts)


def turn_pair(high, low, first, second):
    block = jnp.concatenate([first, second], 0)
    return (dot(high, block, ((1,), (1,))) + dot(low, block, ((1,), (1,)))).astype(BF)


def turn_grads_kernel(*refs):
    *pieces, high, low, out_ref = refs
    seqs, rows, width = pieces[0].shape
    groups, span, _ = high.shape
    for g in range(groups):
        columns = pl.ds(g * span, span)
        for s in range(seqs):
            for k in range(len(pieces) // 2):
                out_ref[s, columns, pl.ds(k * 2 * rows, 2 * rows)] = turn_pair(
                    high[g], low[g], pieces[2 * k][s, :, columns], pieces[2 * k + 1][s, :, columns]
                )


def turn_grads(pieces, parts):
    seqs, rows, width = pieces[0].shape
    shape = jax.ShapeDtypeStruct((seqs, width, len(pieces) * rows), BF)
    return pl.pallas_call(
        turn_grads_kernel,
        in_specs=[VECTORS] * (len(pieces) + 2),
        out_specs=VECTORS,
        out_shape=shape,
        compiler_params=pltpu.CompilerParams(vmem_limit_bytes=limit(shape, shape)),
        name="turn_grads",
    )(*pieces, *parts)


def multiply_kernel(scale, first, second, high, low, grads, acts, out_ref):
    total = None
    for s in range(acts.shape[0]):
        late = turn_pair(high[0], low[0], first[s], second[s])
        corr = dot(jnp.concatenate([grads[s], late], 1), acts[s], ((1,), (0,)))
        total = corr * corr if total is None else total + corr * corr
    out_ref[...] = total * scale


def multiply(last, parts, grads, acts):
    seqs, rows, outs = last[0].shape
    _, length, width = acts.shape
    tile = parts[0].shape[1]
    shape = jax.ShapeDtypeStruct((outs, width), F32)
    return pl.pallas_call(
        functools.partial(multiply_kernel, 1.0 / length),
        grid=(outs // tile,),
        in_specs=[pl.BlockSpec((seqs, rows, tile), lambda i: (0, 0, i))] * 2
        + [pl.BlockSpec((1, tile, tile), lambda i: (i, 0, 0))] * 2
        + [
            pl.BlockSpec((seqs, tile, grads.shape[2]), lambda i: (0, i, 0)),
            pl.BlockSpec((seqs, length, width), lambda i: (0, 0, 0)),
        ],
        out_specs=pl.BlockSpec((tile, width), lambda i: (i, 0)),
        out_shape=shape,
        compiler_params=pltpu.CompilerParams(
            vmem_limit_bytes=limit(acts, jax.ShapeDtypeStruct((seqs, tile, length), BF))
        ),
        name="multiply",
    )(*last, *parts, grads, acts)


def after(value, *earlier):
    return lax.optimization_barrier((value, *earlier))[0]


def shards(acts, grads, act_basis, grad_basis):
    n, m = lax.axis_size("tok"), lax.axis_size("out")
    half = n // 2
    t, q = lax.axis_index("tok"), lax.axis_index("out")
    where = jnp.stack([q, t // 2, t % 2]).astype(jnp.int32)

    def over_y(name, value):
        with jax.named_scope(name):
            return lax.ppermute(value, "tok", [(i, i ^ 1) for i in range(n)])

    def over_z(name, value, shift):
        with jax.named_scope(name):
            return lax.ppermute(
                value, "tok", [(i, (i // 2 + shift) % half * 2 + i % 2) for i in range(n)]
            )

    def over_out(name, value, bit):
        with jax.named_scope(name):
            return lax.ppermute(value, "out", [(i, i ^ bit) for i in range(m)])

    act_parts, grad_parts = spread(act_basis, grad_basis)

    cuts = cut(acts, where, n, m)
    came = [cuts[0]] + [over_z(f"acts_z{k}", cuts[k], k) for k in range(1, half)]
    stay, go = part(came)
    held = {0: [stay, over_y("acts_y", go)]}
    bit = m // 2
    while bit:
        for j, pair in list(held.items()):
            held[j | bit] = [over_out(f"acts_out{j | bit}", v, bit) for v in pair]
        bit //= 2

    ring = {0: grads}
    for k in range(1, (half - 1) // 2 + 1):
        ring[half - k] = over_z(f"grads_z{half - k}", ring[(half - k + 1) % half], -1)
    for k in range(1, half // 2 + 1):
        ring[k] = over_z(f"grads_z{k}", ring[k - 1], 1)
    order = [k for k in range(half) if k != half // 2] + [half // 2]
    pairs = [[ring[k], over_y(f"grads_y{k}", ring[k])] for k in order]

    pieces = [v for j in range(m) for v in held[j]]
    turned_acts = turn_acts(where, pieces, act_parts, order, m)
    turned_grads = turn_grads([v for pair in pairs[:-1] for v in pair], grad_parts)
    return multiply(pairs[-1], grad_parts, turned_grads, turned_acts)


def solution(mesh):
    placed = (
        P(None, "tok", None),
        P(None, "tok", "out"),
        P("tok", None, None),
        P("out", None, None),
    )
    return jax.shard_map(
        shards, mesh=mesh, in_specs=placed, out_specs=P("out", "tok"), check_vma=False
    )
```

```python
import functools

import jax
import jax.numpy as jnp
from jax import lax
from jax.experimental import pallas as pl
from jax.experimental.pallas import tpu as pltpu
from jax.sharding import PartitionSpec as P

BF, F32 = jnp.bfloat16, jnp.float32
SCALARS = pl.BlockSpec(memory_space=pltpu.SMEM)
VECTORS = pl.BlockSpec(memory_space=pltpu.VMEM)


def dot(a, b, contract):
    return lax.dot_general(a, b, (contract, ((), ())), preferred_element_type=F32)


def split(value):
    high = value.astype(BF)
    return high, (value - high.astype(F32)).astype(BF)


def run_all(copies):
    for copy in copies:
        copy.start()
    for copy in copies:
        copy.wait()


def limit(*specs):
    total = sum(2 * s.size * jnp.dtype(s.dtype).itemsize for s in specs)
    return total + 8 * 2**20


def spread_one(transposed, basis_ref, high_ref, low_ref):
    groups, span, _ = high_ref.shape
    blocks = basis_ref.shape[1]
    parts = split(basis_ref[...])
    iota = lambda shape, dim: lax.broadcasted_iota(jnp.int32, shape, dim)
    pq_row, pq_col = (
        (iota((span, 64), 1) % 8, iota((64, span), 0) // 8)
        if transposed
        else (iota((span, 64), 1) // 8, iota((64, span), 0) % 8)
    )
    keep = pq_row == iota((span, 64), 0) % 8
    repeat = (pq_col == iota((64, span), 1) % 8).astype(BF)
    diagonal = iota((span, span), 0) // 8 == iota((span, span), 1) // 8
    for g in range(groups):
        pick = iota((span, blocks), 0) // 8 + g * (span // 8) == iota((span, blocks), 1)
        pick = pick.astype(BF)
        for part, out_ref in zip(parts, (high_ref, low_ref)):
            rows = dot(pick, part, ((1,), (1,)))
            rows = jnp.where(keep, rows, 0.0).astype(BF)
            full = dot(rows, repeat, ((1,), (0,)))
            out_ref[g] = jnp.where(diagonal, full, 0.0).astype(BF)


def spread_kernel(a_ref, g_ref, a_high, a_low, g_high, g_low):
    spread_one(False, a_ref, a_high, a_low)
    spread_one(True, g_ref, g_high, g_low)


def spread(*flat):
    shapes = []
    for basis in flat:
        blocks = basis.shape[1]
        span = min(256, blocks * 8)
        shapes += [jax.ShapeDtypeStruct((blocks * 8 // span, span, span), BF)] * 2
    out = pl.pallas_call(
        spread_kernel,
        out_shape=tuple(shapes),
        compiler_params=pltpu.CompilerParams(vmem_limit_bytes=limit(*shapes)),
        name="spread",
    )(*flat)
    return out[:2], out[2:]


def cut_kernel(half, where_ref, acts_ref, *refs):
    *outs, sems = refs
    q, z, y = where_ref[0], where_ref[1], where_ref[2]
    _, _, quarter, width = outs[0].shape[0:4]
    copies = []
    for k in range(half):
        for other in range(2):
            column = ((z + k) % half * 2 + (y ^ other)) * width
            copies.append(
                pltpu.make_async_copy(
                    acts_ref.at[
                        :,
                        pl.ds(pl.multiple_of(q * quarter, quarter), quarter),
                        pl.ds(pl.multiple_of(column, width), width),
                    ],
                    outs[k].at[other],
                    sems.at[2 * k + other],
                )
            )
    run_all(copies)


def cut(acts, where, n, m):
    seqs, rows, total = acts.shape
    shape = jax.ShapeDtypeStruct((2, seqs, rows // m, total // n), BF)
    return pl.pallas_call(
        functools.partial(cut_kernel, n // 2),
        in_specs=[SCALARS, pl.BlockSpec(memory_space=pltpu.HBM)],
        out_specs=[VECTORS] * (n // 2),
        out_shape=[shape] * (n // 2),
        scratch_shapes=[pltpu.SemaphoreType.DMA((n,))],
        compiler_params=pltpu.CompilerParams(vmem_limit_bytes=limit(*[shape] * (n // 2))),
        name="cut",
    )(where, pltpu.with_memory_space_constraint(acts, pltpu.HBM))


def part_kernel(*refs):
    *pieces, stay, go = refs
    for k, piece in enumerate(pieces):
        stay[k], go[k] = piece[0], piece[1]


def part(pieces):
    half = len(pieces)
    shape = jax.ShapeDtypeStruct((half, *pieces[0].shape[1:]), BF)
    return pl.pallas_call(
        part_kernel,
        in_specs=[VECTORS] * half,
        out_specs=[VECTORS] * 2,
        out_shape=[shape] * 2,
        compiler_params=pltpu.CompilerParams(vmem_limit_bytes=limit(shape, shape)),
        name="part",
    )(*pieces)


def turn_acts_kernel(place_of, m, where_ref, *refs):
    pieces, (high, low, out_ref) = refs[: 2 * m], refs[2 * m :]
    half, seqs, quarter, width = pieces[0].shape
    groups, span, _ = high.shape
    q, z, y = where_ref[0], where_ref[1], where_ref[2]
    for other in range(2):
        starts = [place_of(z, y, lax.rem(z - k + half, half), y ^ other) * m for k in range(half)]
        for j in range(m):
            piece = pieces[2 * j + other]
            for g in range(groups):
                columns = pl.ds(g * span, span)
                block = piece[:, :, :, columns].reshape(half * seqs * quarter, span)
                turned = dot(block, high[g], ((1,), (0,))) + dot(block, low[g], ((1,), (0,)))
                turned = turned.astype(BF).reshape(half, seqs, quarter, span)
                for k in range(half):
                    start = pl.multiple_of((starts[k] + (q ^ j)) * quarter, quarter)
                    out_ref[:, pl.ds(start, quarter), columns] = turned[k]


def turn_acts(where, pieces, parts, place_of, m):
    half, seqs, quarter, width = pieces[0].shape
    shape = jax.ShapeDtypeStruct((seqs, 2 * half * m * quarter, width), BF)
    return pl.pallas_call(
        functools.partial(turn_acts_kernel, place_of, m),
        in_specs=[SCALARS] + [VECTORS] * (2 * m + 2),
        out_specs=VECTORS,
        out_shape=shape,
        compiler_params=pltpu.CompilerParams(vmem_limit_bytes=limit(shape, shape)),
        name="turn_acts",
    )(where, *pieces, *parts)


def turn_pair(high, low, first, second):
    block = jnp.concatenate([first, second], 0)
    return (dot(high, block, ((1,), (1,))) + dot(low, block, ((1,), (1,)))).astype(BF)


def turn_grads_kernel(*refs):
    *pieces, high, low, out_ref = refs
    seqs, rows, width = pieces[0].shape
    groups, span, _ = high.shape
    for g in range(groups):
        columns = pl.ds(g * span, span)
        for s in range(seqs):
            for k in range(len(pieces) // 2):
                out_ref[s, columns, pl.ds(k * 2 * rows, 2 * rows)] = turn_pair(
                    high[g], low[g], pieces[2 * k][s, :, columns], pieces[2 * k + 1][s, :, columns]
                )


def turn_grads(pieces, parts):
    seqs, rows, width = pieces[0].shape
    shape = jax.ShapeDtypeStruct((seqs, width, len(pieces) * rows), BF)
    return pl.pallas_call(
        turn_grads_kernel,
        in_specs=[VECTORS] * (len(pieces) + 2),
        out_specs=VECTORS,
        out_shape=shape,
        compiler_params=pltpu.CompilerParams(vmem_limit_bytes=limit(shape, shape)),
        name="turn_grads",
    )(*pieces, *parts)


def multiply_kernel(scale, first, second, high, low, grads, acts, *refs):
    *before, out_ref = refs
    total = before[0][...] if before else None
    for s in range(acts.shape[0]):
        late = turn_pair(high[0], low[0], first[s], second[s])
        corr = dot(jnp.concatenate([grads[s], late], 1), acts[s], ((1,), (0,)))
        square = corr * corr * scale
        total = square if total is None else total + square
    out_ref[...] = total


def multiply(begin, last, parts, grads, acts, before=()):
    count, rows, outs = last[1].shape
    seqs, length, width = acts.shape
    tile = parts[0].shape[1]
    shape = jax.ShapeDtypeStruct((outs, width), F32)
    at = begin // count
    assert at * count == begin
    strip = pl.BlockSpec((tile, width), lambda i: (i, 0))
    return pl.pallas_call(
        functools.partial(multiply_kernel, 1.0 / length),
        grid=(outs // tile,),
        in_specs=[
            pl.BlockSpec((count, rows, tile), lambda i: (0, 0, i)),
            pl.BlockSpec((count, rows, tile), lambda i: (0, 0, i)),
        ]
        + [pl.BlockSpec((1, tile, tile), lambda i: (i, 0, 0))] * 2
        + [
            pl.BlockSpec((count, tile, grads.shape[2]), lambda i: (at, i, 0)),
            pl.BlockSpec((count, length, width), lambda i: (at, 0, 0)),
        ]
        + [strip] * len(before),
        out_specs=strip,
        out_shape=shape,
        compiler_params=pltpu.CompilerParams(
            vmem_limit_bytes=limit(acts, jax.ShapeDtypeStruct((seqs, tile, length), BF))
        ),
        name="multiply",
    )(*last, *parts, grads, acts, *before)


def after(value, *earlier):
    return lax.optimization_barrier((value, *earlier))[0]


CAME = ("az1", "az2", "az3")
TIES = {
    "u2": CAME,
    "d2": CAME,
    "u3": ("ay", "as2"),
    "d3": ("ay", "spread"),
    "u": ("ag2", "as1"),
    "d": ("tg",),
}


def shards(acts, grads, act_basis, grad_basis):
    n, m = lax.axis_size("tok"), lax.axis_size("out")
    half, seqs = n // 2, acts.shape[0]
    t, q = lax.axis_index("tok"), lax.axis_index("out")
    where = jnp.stack([q, t // 2, t % 2]).astype(jnp.int32)
    ops, done = {}, {}

    def get(name):
        if name not in done:
            earlier = [get(e) for e in TIES.get(name, ()) if e in ops]
            done[name] = ops[name](lambda v: after(v, *earlier) if earlier else v)
        return done[name]

    def send(name, source, axis, perm):
        def run(tie):
            value = tie(source())
            with jax.named_scope(name):
                return lax.ppermute(value, axis, perm)

        ops[name] = run

    def over_y(name, source):
        send(name, source, "tok", [(i, i ^ 1) for i in range(n)])

    def over_z(name, source, shift):
        send(name, source, "tok", [(i, (i // 2 + shift) % half * 2 + i % 2) for i in range(n)])

    def over_out(name, source, bit):
        send(name, source, "out", [(i, i ^ bit) for i in range(m)])

    flat = [jnp.transpose(b, (1, 2, 0)).reshape(64, -1) for b in (act_basis, grad_basis)]
    ops["spread"] = lambda tie: spread(tie(flat[0]), flat[1])
    ops["cut"] = lambda tie: cut(tie(acts), where, n, m)

    for k in range(1, half):
        over_z(f"az{k}", lambda k=k: get("cut")[k], k)
    ops["part"] = lambda tie: part([get("cut")[0]] + [get(f"az{k}") for k in range(1, half)])
    over_y("ay", lambda: get("part")[1])
    ops["as0"] = lambda tie: get("part")[0]
    ops["ag0"] = lambda tie: get("ay")
    for letter in "sg":
        bit = m // 2
        held = [0]
        while bit:
            for j in list(held):
                held.append(j | bit)
                over_out(f"a{letter}{j | bit}", lambda x=f"a{letter}{j}": get(x), bit)
            bit //= 2

    ring = [2 * z for z in range(half)] + [2 * z + 1 for z in reversed(range(half))]

    def round_ring(name, source, step):
        perm = [(ring[i], ring[(i + step) % n]) for i in range(n)]
        send(name, source, "tok", sorted(perm))

    first = seqs - 1
    ops["u0"] = ops["d0"] = lambda tie: grads
    for i in range(1, half):
        for way, step in (("u", 1), ("d", -1)):
            round_ring(f"{way}{i}", lambda way=way, i=i: get(f"{way}{i - 1}"), step)
    round_ring("u", lambda: get(f"u{half - 1}")[:first], 1)
    round_ring("d", lambda: get(f"d{half - 1}")[first:], -1)

    names = ["u0"] + [f"{way}{i}" for i in range(1, half) for way in "ud"]

    def place_of(z, y, from_z, from_y):
        mine = jnp.where(y == 0, z, n - 1 - z)
        other = jnp.where(from_y == 0, from_z, n - 1 - from_z)
        ahead = lax.rem(mine - other + n, n)
        return jnp.where(
            ahead == 0, 0, jnp.where(ahead <= half, 2 * ahead - 1, 2 * (n - ahead))
        )

    ops["ta"] = lambda tie: turn_acts(
        where,
        [get(f"a{letter}{j}") for j in range(m) for letter in "sg"],
        get("spread")[0],
        place_of,
        m,
    )
    ops["tg"] = lambda tie: turn_grads([get(x) for x in names[:-1]], get("spread")[1])
    late = get(names[-1])
    total = ()
    for last, part_of, lo in ((get("u"), late[:first], 0), (get("d"), late[first:], first)):
        total = (multiply(lo, [part_of, last], get("spread")[1], get("tg"), get("ta"), total),)
    return total[0]


def solution(mesh):
    placed = (
        P(None, "tok", None),
        P(None, "tok", "out"),
        P("tok", None, None),
        P("out", None, None),
    )
    return jax.shard_map(
        shards, mesh=mesh, in_specs=placed, out_specs=P("out", "tok"), check_vma=False
    )
```

```python
import functools

import jax
import jax.numpy as jnp
from jax import lax
from jax.experimental import pallas as pl
from jax.experimental.pallas import tpu as pltpu
from jax.sharding import PartitionSpec as P

BF, F32 = jnp.bfloat16, jnp.float32
COSTS = {'turn_grads': 10000000000}


def cost(name):
    flops = COSTS.get(name)
    return flops and pl.CostEstimate(flops=flops, bytes_accessed=0, transcendentals=0)

SCALARS = pl.BlockSpec(memory_space=pltpu.SMEM)
VECTORS = pl.BlockSpec(memory_space=pltpu.VMEM)


def dot(a, b, contract):
    return lax.dot_general(a, b, (contract, ((), ())), preferred_element_type=F32)


def split(value):
    high = value.astype(BF)
    return high, (value - high.astype(F32)).astype(BF)


def run_all(copies):
    for copy in copies:
        copy.start()
    for copy in copies:
        copy.wait()


def limit(*specs):
    total = sum(2 * s.size * jnp.dtype(s.dtype).itemsize for s in specs)
    return total + 8 * 2**20


def spread_one(transposed, basis_ref, high_ref, low_ref):
    groups, span, _ = high_ref.shape
    blocks = basis_ref.shape[1]
    parts = split(basis_ref[...])
    iota = lambda shape, dim: lax.broadcasted_iota(jnp.int32, shape, dim)
    pq_row, pq_col = (
        (iota((span, 64), 1) % 8, iota((64, span), 0) // 8)
        if transposed
        else (iota((span, 64), 1) // 8, iota((64, span), 0) % 8)
    )
    keep = pq_row == iota((span, 64), 0) % 8
    repeat = (pq_col == iota((64, span), 1) % 8).astype(BF)
    diagonal = iota((span, span), 0) // 8 == iota((span, span), 1) // 8
    for g in range(groups):
        pick = iota((span, blocks), 0) // 8 + g * (span // 8) == iota((span, blocks), 1)
        pick = pick.astype(BF)
        for part, out_ref in zip(parts, (high_ref, low_ref)):
            rows = dot(pick, part, ((1,), (1,)))
            rows = jnp.where(keep, rows, 0.0).astype(BF)
            full = dot(rows, repeat, ((1,), (0,)))
            out_ref[g] = jnp.where(diagonal, full, 0.0).astype(BF)


def spread_kernel(a_ref, g_ref, a_high, a_low, g_high, g_low):
    spread_one(False, a_ref, a_high, a_low)
    spread_one(True, g_ref, g_high, g_low)


def spread(*flat):
    shapes = []
    for basis in flat:
        blocks = basis.shape[1]
        span = min(256, blocks * 8)
        shapes += [jax.ShapeDtypeStruct((blocks * 8 // span, span, span), BF)] * 2
    out = pl.pallas_call(
        spread_kernel,
        out_shape=tuple(shapes),
        compiler_params=pltpu.CompilerParams(vmem_limit_bytes=limit(*shapes)),
        cost_estimate=cost("spread"),
        name="spread",
    )(*flat)
    return out[:2], out[2:]


def cut_kernel(where_ref, acts_ref, stay_ref, go_ref, sems):
    half, _, quarter, width = stay_ref.shape
    q, z, y = where_ref[0], where_ref[1], where_ref[2]
    rows = pl.ds(pl.multiple_of(q * quarter, quarter), quarter)
    copies = []
    for k in range(half):
        for other, out_ref in enumerate((stay_ref, go_ref)):
            column = pl.multiple_of((lax.rem(z + k, half) * 2 + (y ^ other)) * width, width)
            copies.append(
                pltpu.make_async_copy(
                    acts_ref.at[:, rows, pl.ds(column, width)],
                    out_ref.at[k],
                    sems.at[2 * k + other],
                )
            )
    run_all(copies)


def cut(acts, where, n, m):
    seqs, rows, total = acts.shape
    shape = jax.ShapeDtypeStruct((n // 2, seqs, rows // m, total // n), BF)
    return pl.pallas_call(
        cut_kernel,
        in_specs=[SCALARS, pl.BlockSpec(memory_space=pltpu.HBM)],
        out_specs=[VECTORS] * 2,
        out_shape=[shape] * 2,
        scratch_shapes=[pltpu.SemaphoreType.DMA((n,))],
        compiler_params=pltpu.CompilerParams(vmem_limit_bytes=limit(shape, shape)),
        cost_estimate=cost("cut"),
        name="cut",
    )(where, pltpu.with_memory_space_constraint(acts, pltpu.HBM))


def pair_kernel(stay, came, *outs):
    for k, out in enumerate(outs):
        out[0], out[1] = stay[k], came[k]


def pair(stay, came):
    half = stay.shape[0]
    shape = jax.ShapeDtypeStruct((2, *stay.shape[1:]), BF)
    return pl.pallas_call(
        pair_kernel,
        in_specs=[VECTORS] * 2,
        out_specs=[VECTORS] * half,
        out_shape=[shape] * half,
        compiler_params=pltpu.CompilerParams(vmem_limit_bytes=limit(*[shape] * half)),
        cost_estimate=cost("pair"),
        name="pair",
    )(stay, came)


def join_kernel(*refs):
    *pieces, out = refs
    begin = 0
    for piece in pieces:
        out[begin : begin + piece.shape[0]] = piece[...]
        begin += piece.shape[0]


def join(pieces):
    count = sum(p.shape[0] for p in pieces)
    shape = jax.ShapeDtypeStruct((count, *pieces[0].shape[1:]), BF)
    return pl.pallas_call(
        join_kernel,
        in_specs=[VECTORS] * len(pieces),
        out_specs=VECTORS,
        out_shape=shape,
        compiler_params=pltpu.CompilerParams(vmem_limit_bytes=limit(shape, shape)),
        cost_estimate=cost("join"),
        name="join",
    )(*pieces)


def turn_acts_kernel(place_of, half, m, content, where_ref, *refs):
    *pieces, high, low, out_ref = refs
    groups, span, _ = high.shape
    q, z, y = where_ref[0], where_ref[1], where_ref[2]
    seqs, quarter, width = pieces[0].shape[1:]
    start_of = {}
    for piece, blocks in zip(pieces, content):
        for j, k, other in blocks:
            if (k, other) not in start_of:
                place = place_of(z, y, lax.rem(z - k + half, half), y ^ other)
                start_of[k, other] = place * m
        for g in range(groups):
            columns = pl.ds(g * span, span)
            block = piece[:, :, :, columns].reshape(len(blocks) * seqs * quarter, span)
            turned = dot(block, high[g], ((1,), (0,))) + dot(block, low[g], ((1,), (0,)))
            turned = turned.astype(BF).reshape(len(blocks), seqs, quarter, span)
            for i, (j, k, other) in enumerate(blocks):
                start = pl.multiple_of((start_of[k, other] + (q ^ j)) * quarter, quarter)
                out_ref[:, pl.ds(start, quarter), columns] = turned[i]


def turn_acts(where, pieces, content, parts, place_of, half, m):
    seqs, quarter, width = pieces[0].shape[1:]
    shape = jax.ShapeDtypeStruct((seqs, 2 * half * m * quarter, width), BF)
    return pl.pallas_call(
        functools.partial(turn_acts_kernel, place_of, half, m, content),
        in_specs=[SCALARS] + [VECTORS] * (len(pieces) + 2),
        out_specs=VECTORS,
        out_shape=shape,
        compiler_params=pltpu.CompilerParams(vmem_limit_bytes=limit(shape, shape)),
        cost_estimate=cost("turn_acts"),
        name="turn_acts",
    )(where, *pieces, *parts)


def turn_pair(high, low, first, second):
    block = jnp.concatenate([first, second], 0)
    return (dot(high, block, ((1,), (1,))) + dot(low, block, ((1,), (1,)))).astype(BF)


def turn_grads_kernel(*refs):
    *pieces, high, low, out_ref = refs
    seqs, rows, width = pieces[0].shape
    groups, span, _ = high.shape
    for g in range(groups):
        columns = pl.ds(g * span, span)
        for s in range(seqs):
            for k in range(len(pieces) // 2):
                out_ref[s, columns, pl.ds(k * 2 * rows, 2 * rows)] = turn_pair(
                    high[g], low[g], pieces[2 * k][s, :, columns], pieces[2 * k + 1][s, :, columns]
                )


def turn_grads(pieces, parts):
    seqs, rows, width = pieces[0].shape
    shape = jax.ShapeDtypeStruct((seqs, width, len(pieces) * rows), BF)
    return pl.pallas_call(
        turn_grads_kernel,
        in_specs=[VECTORS] * (len(pieces) + 2),
        out_specs=VECTORS,
        out_shape=shape,
        compiler_params=pltpu.CompilerParams(vmem_limit_bytes=limit(shape, shape)),
        cost_estimate=cost("turn_grads"),
        name="turn_grads",
    )(*pieces, *parts)


def multiply_kernel(scale, begin, count, first, second, high, low, acts, *refs):
    grads, before, out_ref = refs[:count], refs[count:-1], refs[-1]
    step = pl.program_id(0)
    tile = high.shape[1]
    columns = pl.ds(pl.multiple_of(step * tile, tile), tile)
    total = before[0][columns, :] if before else None
    for i in range(second.shape[0]):
        s = begin + i
        late = turn_pair(high[step], low[step], first[s, :, columns], second[i, :, columns])
        turned = jnp.concatenate([*(g[s, columns, :] for g in grads), late], 1)
        corr = dot(turned, acts[s], ((1,), (0,)))
        square = corr * corr * scale
        total = square if total is None else total + square
    out_ref[(columns if out_ref.shape[0] > tile else slice(None)), :] = total


def multiply(begin, last, parts, grads, acts, before=()):
    outs = last[1].shape[2]
    _, length, width = acts.shape
    tile = parts[0].shape[1]
    shape = jax.ShapeDtypeStruct((outs, width), F32)
    strip = pl.BlockSpec((tile, width), lambda i: (i, 0))
    return pl.pallas_call(
        functools.partial(multiply_kernel, 1.0 / length, begin, len(grads)),
        grid=(outs // tile,),
        in_specs=[VECTORS] * (5 + len(grads) + len(before)),
        out_specs=strip if before else VECTORS,
        out_shape=shape,
        compiler_params=pltpu.CompilerParams(vmem_limit_bytes=limit(shape, shape)),
        cost_estimate=cost("multiply"),
        name="multiply",
    )(*last, *parts, acts, *grads, *before)


def after(value, *earlier):
    return lax.optimization_barrier((value, *earlier))[0]


TIES = {'x22': ('u2', 'd2'), 'x12': ('x02',), 'az2': ('u1', 'd1'), 'u3': ('x12',)}


def shards(acts, grads, act_basis, grad_basis):
    n, m = lax.axis_size("tok"), lax.axis_size("out")
    half, seqs = n // 2, acts.shape[0]
    t, q = lax.axis_index("tok"), lax.axis_index("out")
    where = jnp.stack([q, t // 2, t % 2]).astype(jnp.int32)
    ops, done = {}, {}

    def get(name):
        if name not in done:
            earlier = [get(e) for e in TIES.get(name, ()) if e in ops]
            done[name] = ops[name](lambda v: after(v, *earlier) if earlier else v)
        return done[name]

    def send(name, source, axis, perm):
        def run(tie):
            value = tie(source())
            with jax.named_scope(name):
                return lax.ppermute(value, axis, perm)

        ops[name] = run

    def over_y(name, source):
        send(name, source, "tok", [(i, i ^ 1) for i in range(n)])

    def over_z(name, source, shift):
        send(name, source, "tok", [(i, (i // 2 + shift) % half * 2 + i % 2) for i in range(n)])

    def over_out(name, source, bit):
        send(name, source, "out", [(i, i ^ bit) for i in range(m)])

    flat = [jnp.transpose(b, (1, 2, 0)).reshape(64, -1) for b in (act_basis, grad_basis)]
    ops["spread"] = lambda tie: spread(tie(flat[0]), flat[1])
    ops["cut"] = lambda tie: cut(tie(acts), where, n, m)

    over_y("ay", lambda: get("cut")[1])
    ops["pair"] = lambda tie: pair(get("cut")[0], get("ay"))
    for k in range(1, half):
        over_z(f"az{k}", lambda k=k: get("pair")[k], k)
    come = lambda k: get(f"az{k}") if k else get("pair")[0]
    pieces, content = [], []
    middle = half // 2
    for g, ks in enumerate(([0], [k for k in range(1, half) if k != middle], [middle])):
        held = f"g{g}"
        blocks = [(0, k, other) for k in ks for other in range(2)]
        ops[held] = lambda tie, ks=ks: join([come(k) for k in ks]) if len(ks) > 1 else come(ks[0])
        bit = m // 2
        while bit:
            got = f"x{g}{bit}"
            over_out(got, lambda held=held: get(held), bit)
            theirs = [(j ^ bit, k, other) for j, k, other in blocks]
            bit //= 2
            if not bit:
                pieces.append(got)
                content.append(theirs)
                break
            both = f"{held}+"
            ops[both] = lambda tie, held=held, got=got: join([get(held), get(got)])
            held, blocks = both, blocks + theirs
        pieces.append(held)
        content.append(blocks)

    ring = [2 * z for z in range(half)] + [2 * z + 1 for z in reversed(range(half))]

    def round_ring(name, source, step):
        perm = [(ring[i], ring[(i + step) % n]) for i in range(n)]
        send(name, source, "tok", sorted(perm))

    first = seqs - 1
    ops["u0"] = ops["d0"] = lambda tie: grads
    for i in range(1, half):
        for way, step in (("u", 1), ("d", -1)):
            round_ring(f"{way}{i}", lambda way=way, i=i: get(f"{way}{i - 1}"), step)
    round_ring("u", lambda: get(f"u{half - 1}")[:first], 1)
    round_ring("d", lambda: get(f"d{half - 1}")[first:], -1)

    names = ["u0"] + [f"{way}{i}" for i in range(1, half) for way in "ud"]

    def place_of(z, y, from_z, from_y):
        mine = jnp.where(y == 0, z, n - 1 - z)
        other = jnp.where(from_y == 0, from_z, n - 1 - from_z)
        ahead = lax.rem(mine - other + n, n)
        return jnp.where(
            ahead == 0, 0, jnp.where(ahead <= half, 2 * ahead - 1, 2 * (n - ahead))
        )

    ops["ta"] = lambda tie: turn_acts(
        tie(where), [get(x) for x in pieces], content, get("spread")[0], place_of, half, m
    )
    turned = {"tg1": names[:-3], "tg2": names[-3:-1]}
    for name, of in turned.items():
        ops[name] = lambda tie, of=of: turn_grads(
            [tie(get(of[0]))] + [get(x) for x in of[1:]], get("spread")[1]
        )
    late = get(names[-1])
    total = ()
    for name, lo in (("d", first), ("u", 0)):
        last = [late, get(name)]
        total = (multiply(lo, last, get("spread")[1], [get(x) for x in turned], get("ta"), total),)
    return total[0]


def solution(mesh):
    placed = (
        P(None, "tok", None),
        P(None, "tok", "out"),
        P("tok", None, None),
        P("out", None, None),
    )
    return jax.shard_map(
        shards, mesh=mesh, in_specs=placed, out_specs=P("out", "tok"), check_vma=False
    )
```

```python
import functools

import jax
import jax.numpy as jnp
from jax import lax
from jax.experimental import pallas as pl
from jax.experimental.pallas import tpu as pltpu
from jax.sharding import PartitionSpec as P

BF, F32 = jnp.bfloat16, jnp.float32
COSTS = {'tg1': 10000000000, 'tg2': 10000000000}


def cost(name):
    flops = COSTS.get(name)
    return flops and pl.CostEstimate(flops=flops, bytes_accessed=0, transcendentals=0)

SCALARS = pl.BlockSpec(memory_space=pltpu.SMEM)
VECTORS = pl.BlockSpec(memory_space=pltpu.VMEM)


def dot(a, b, contract):
    return lax.dot_general(a, b, (contract, ((), ())), preferred_element_type=F32)


def split(value):
    high = value.astype(BF)
    return high, (value - high.astype(F32)).astype(BF)


def run_all(copies):
    for copy in copies:
        copy.start()
    for copy in copies:
        copy.wait()


def limit(*specs):
    total = sum(2 * s.size * jnp.dtype(s.dtype).itemsize for s in specs)
    return total + 8 * 2**20


def spread_one(transposed, basis_ref, high_ref, low_ref):
    groups, span, _ = high_ref.shape
    blocks = basis_ref.shape[1]
    parts = split(basis_ref[...])
    iota = lambda shape, dim: lax.broadcasted_iota(jnp.int32, shape, dim)
    pq_row, pq_col = (
        (iota((span, 64), 1) % 8, iota((64, span), 0) // 8)
        if transposed
        else (iota((span, 64), 1) // 8, iota((64, span), 0) % 8)
    )
    keep = pq_row == iota((span, 64), 0) % 8
    repeat = (pq_col == iota((64, span), 1) % 8).astype(BF)
    diagonal = iota((span, span), 0) // 8 == iota((span, span), 1) // 8
    for g in range(groups):
        pick = iota((span, blocks), 0) // 8 + g * (span // 8) == iota((span, blocks), 1)
        pick = pick.astype(BF)
        for part, out_ref in zip(parts, (high_ref, low_ref)):
            rows = dot(pick, part, ((1,), (1,)))
            rows = jnp.where(keep, rows, 0.0).astype(BF)
            full = dot(rows, repeat, ((1,), (0,)))
            out_ref[g] = jnp.where(diagonal, full, 0.0).astype(BF)


def spread_kernel(a_ref, g_ref, a_high, a_low, g_high, g_low):
    spread_one(False, a_ref, a_high, a_low)
    spread_one(True, g_ref, g_high, g_low)


def spread(*flat):
    shapes = []
    for basis in flat:
        blocks = basis.shape[1]
        span = min(256, blocks * 8)
        shapes += [jax.ShapeDtypeStruct((blocks * 8 // span, span, span), BF)] * 2
    out = pl.pallas_call(
        spread_kernel,
        out_shape=tuple(shapes),
        compiler_params=pltpu.CompilerParams(vmem_limit_bytes=limit(*shapes)),
        cost_estimate=cost("spread"),
        name="spread",
    )(*flat)
    return out[:2], out[2:]


def cut_kernel(where_ref, acts_ref, stay_ref, go_ref, sems):
    half, _, quarter, width = stay_ref.shape
    q, z, y = where_ref[0], where_ref[1], where_ref[2]
    rows = pl.ds(pl.multiple_of(q * quarter, quarter), quarter)
    copies = []
    for k in range(half):
        for other, out_ref in enumerate((stay_ref, go_ref)):
            column = pl.multiple_of((lax.rem(z + k, half) * 2 + (y ^ other)) * width, width)
            copies.append(
                pltpu.make_async_copy(
                    acts_ref.at[:, rows, pl.ds(column, width)],
                    out_ref.at[k],
                    sems.at[2 * k + other],
                )
            )
    run_all(copies)


def cut(acts, where, n, m):
    seqs, rows, total = acts.shape
    shape = jax.ShapeDtypeStruct((n // 2, seqs, rows // m, total // n), BF)
    return pl.pallas_call(
        cut_kernel,
        in_specs=[SCALARS, pl.BlockSpec(memory_space=pltpu.HBM)],
        out_specs=[VECTORS] * 2,
        out_shape=[shape] * 2,
        scratch_shapes=[pltpu.SemaphoreType.DMA((n,))],
        compiler_params=pltpu.CompilerParams(vmem_limit_bytes=limit(shape, shape)),
        cost_estimate=cost("cut"),
        name="cut",
    )(where, pltpu.with_memory_space_constraint(acts, pltpu.HBM))


def pair_kernel(stay, came, *outs):
    for k, out in enumerate(outs):
        out[0], out[1] = stay[k], came[k]


def pair(stay, came):
    half = stay.shape[0]
    shape = jax.ShapeDtypeStruct((2, *stay.shape[1:]), BF)
    return pl.pallas_call(
        pair_kernel,
        in_specs=[VECTORS] * 2,
        out_specs=[VECTORS] * half,
        out_shape=[shape] * half,
        compiler_params=pltpu.CompilerParams(vmem_limit_bytes=limit(*[shape] * half)),
        cost_estimate=cost("pair"),
        name="pair",
    )(stay, came)


def join_kernel(*refs):
    *pieces, out = refs
    begin = 0
    for piece in pieces:
        out[begin : begin + piece.shape[0]] = piece[...]
        begin += piece.shape[0]


def join(pieces):
    count = sum(p.shape[0] for p in pieces)
    shape = jax.ShapeDtypeStruct((count, *pieces[0].shape[1:]), BF)
    return pl.pallas_call(
        join_kernel,
        in_specs=[VECTORS] * len(pieces),
        out_specs=VECTORS,
        out_shape=shape,
        compiler_params=pltpu.CompilerParams(vmem_limit_bytes=limit(shape, shape)),
        cost_estimate=cost("join"),
        name="join",
    )(*pieces)


def turn_acts_kernel(place_of, half, m, content, where_ref, *refs):
    *pieces, high, low, out_ref = refs
    groups, span, _ = high.shape
    q, z, y = where_ref[0], where_ref[1], where_ref[2]
    seqs, quarter, width = pieces[0].shape[1:]
    start_of = {}
    for piece, blocks in zip(pieces, content):
        for j, k, other in blocks:
            if (k, other) not in start_of:
                place = place_of(z, y, lax.rem(z - k + half, half), y ^ other)
                start_of[k, other] = place * m
        for g in range(groups):
            columns = pl.ds(g * span, span)
            block = piece[:, :, :, columns].reshape(len(blocks) * seqs * quarter, span)
            turned = dot(block, high[g], ((1,), (0,))) + dot(block, low[g], ((1,), (0,)))
            turned = turned.astype(BF).reshape(len(blocks), seqs, quarter, span)
            for i, (j, k, other) in enumerate(blocks):
                start = pl.multiple_of((start_of[k, other] + (q ^ j)) * quarter, quarter)
                out_ref[:, pl.ds(start, quarter), columns] = turned[i]


def turn_acts(where, pieces, content, parts, place_of, half, m):
    seqs, quarter, width = pieces[0].shape[1:]
    shape = jax.ShapeDtypeStruct((seqs, 2 * half * m * quarter, width), BF)
    return pl.pallas_call(
        functools.partial(turn_acts_kernel, place_of, half, m, content),
        in_specs=[SCALARS] + [VECTORS] * (len(pieces) + 2),
        out_specs=VECTORS,
        out_shape=shape,
        compiler_params=pltpu.CompilerParams(vmem_limit_bytes=limit(shape, shape)),
        cost_estimate=cost("turn_acts"),
        name="turn_acts",
    )(where, *pieces, *parts)


def turn_pair(high, low, first, second):
    block = jnp.concatenate([first, second], 0)
    return (dot(high, block, ((1,), (1,))) + dot(low, block, ((1,), (1,)))).astype(BF)


def turn_grads_kernel(*refs):
    *pieces, high, low, out_ref = refs
    seqs, rows, width = pieces[0].shape
    groups, span, _ = high.shape
    for g in range(groups):
        columns = pl.ds(g * span, span)
        for s in range(seqs):
            for k in range(len(pieces) // 2):
                out_ref[s, columns, pl.ds(k * 2 * rows, 2 * rows)] = turn_pair(
                    high[g], low[g], pieces[2 * k][s, :, columns], pieces[2 * k + 1][s, :, columns]
                )


def turn_grads(name, pieces, parts):
    seqs, rows, width = pieces[0].shape
    shape = jax.ShapeDtypeStruct((seqs, width, len(pieces) * rows), BF)
    return pl.pallas_call(
        turn_grads_kernel,
        in_specs=[VECTORS] * (len(pieces) + 2),
        out_specs=VECTORS,
        out_shape=shape,
        compiler_params=pltpu.CompilerParams(vmem_limit_bytes=limit(shape, shape)),
        cost_estimate=cost(name),
        name="turn_grads",
    )(*pieces, *parts)


def multiply_kernel(scale, begin, count, first, second, high, low, acts, *refs):
    grads, before, out_ref = refs[:count], refs[count:-1], refs[-1]
    step = pl.program_id(0)
    tile, width = high.shape[1], acts.shape[2]
    columns = pl.ds(pl.multiple_of(step * tile, tile), tile)
    turned = []
    for i in range(second.shape[0]):
        s = begin + i
        late = turn_pair(high[step], low[step], first[s, :, columns], second[i, :, columns])
        turned.append(jnp.concatenate([*(g[s, columns, :] for g in grads), late], 1))
    for c in range(0, width, min(512, width)):
        for r in range(0, tile, 256):
            to = pl.ds(c, min(512, width))
            total = None
            for i in range(second.shape[0]):
                corr = dot(turned[i][r : r + 256], acts[begin + i, :, to], ((1,), (0,)))
                total = corr * corr if total is None else total + corr * corr
            total = total * scale
            rows = pl.ds(pl.multiple_of(step * tile + r, 256), 256)
            if before:
                out_ref[r : r + 256, to] = total + before[0][rows, to]
            else:
                out_ref[rows, to] = total


def multiply(begin, last, parts, grads, acts, before=()):
    outs = last[1].shape[2]
    _, length, width = acts.shape
    tile = parts[0].shape[1]
    shape = jax.ShapeDtypeStruct((outs, width), F32)
    strip = pl.BlockSpec((tile, width), lambda i: (i, 0))
    return pl.pallas_call(
        functools.partial(multiply_kernel, 1.0 / length, begin, len(grads)),
        grid=(outs // tile,),
        in_specs=[VECTORS] * (5 + len(grads) + len(before)),
        out_specs=strip if before else VECTORS,
        out_shape=shape,
        compiler_params=pltpu.CompilerParams(vmem_limit_bytes=limit(shape, shape)),
        cost_estimate=cost("multiply"),
        name="multiply",
    )(*last, *parts, acts, *grads, *before)


def after(value, *earlier):
    return lax.optimization_barrier((value, *earlier))[0]


TIES = {'az1': ('u1', 'd1'), 'az3': ('u1', 'd1'), 'az2': ('d2',), 'x12': ('x02',), 'x22': ('u2',)}


def shards(acts, grads, act_basis, grad_basis):
    n, m = lax.axis_size("tok"), lax.axis_size("out")
    half, seqs = n // 2, acts.shape[0]
    t, q = lax.axis_index("tok"), lax.axis_index("out")
    where = jnp.stack([q, t // 2, t % 2]).astype(jnp.int32)
    ops, done = {}, {}

    def get(name):
        if name not in done:
            earlier = [get(e) for e in TIES.get(name, ()) if e in ops]
            done[name] = ops[name](lambda v: after(v, *earlier) if earlier else v)
        return done[name]

    def send(name, source, axis, perm):
        def run(tie):
            value = tie(source())
            with jax.named_scope(name):
                return lax.ppermute(value, axis, perm)

        ops[name] = run

    def over_y(name, source):
        send(name, source, "tok", [(i, i ^ 1) for i in range(n)])

    def over_z(name, source, shift):
        send(name, source, "tok", [(i, (i // 2 + shift) % half * 2 + i % 2) for i in range(n)])

    def over_out(name, source, bit):
        send(name, source, "out", [(i, i ^ bit) for i in range(m)])

    flat = [jnp.transpose(b, (1, 2, 0)).reshape(64, -1) for b in (act_basis, grad_basis)]
    ops["spread"] = lambda tie: spread(tie(flat[0]), flat[1])
    ops["cut"] = lambda tie: cut(tie(acts), where, n, m)

    over_y("ay", lambda: get("cut")[1])
    ops["pair"] = lambda tie: pair(get("cut")[0], get("ay"))
    for k in range(1, half):
        over_z(f"az{k}", lambda k=k: get("pair")[k], k)
    come = lambda k: get(f"az{k}") if k else get("pair")[0]
    pieces, content = [], []
    middle = half // 2
    for g, ks in enumerate(([0], [k for k in range(1, half) if k != middle], [middle])):
        held = f"g{g}"
        blocks = [(0, k, other) for k in ks for other in range(2)]
        ops[held] = lambda tie, ks=ks: join([come(k) for k in ks]) if len(ks) > 1 else come(ks[0])
        bit = m // 2
        while bit:
            got = f"x{g}{bit}"
            over_out(got, lambda held=held: get(held), bit)
            theirs = [(j ^ bit, k, other) for j, k, other in blocks]
            bit //= 2
            if not bit:
                pieces.append(got)
                content.append(theirs)
                break
            both = f"{held}+"
            ops[both] = lambda tie, held=held, got=got: join([get(held), get(got)])
            held, blocks = both, blocks + theirs
        pieces.append(held)
        content.append(blocks)

    ring = [2 * z for z in range(half)] + [2 * z + 1 for z in reversed(range(half))]

    def round_ring(name, source, step):
        perm = [(ring[i], ring[(i + step) % n]) for i in range(n)]
        send(name, source, "tok", sorted(perm))

    first = seqs - 1
    ops["u0"] = ops["d0"] = lambda tie: grads
    for i in range(1, half):
        for way, step in (("u", 1), ("d", -1)):
            round_ring(f"{way}{i}", lambda way=way, i=i: get(f"{way}{i - 1}"), step)
    round_ring("u", lambda: get(f"u{half - 1}")[:first], 1)
    round_ring("d", lambda: get(f"d{half - 1}")[first:], -1)

    names = ["u0"] + [f"{way}{i}" for i in range(1, half) for way in "ud"]

    def place_of(z, y, from_z, from_y):
        mine = jnp.where(y == 0, z, n - 1 - z)
        other = jnp.where(from_y == 0, from_z, n - 1 - from_z)
        ahead = lax.rem(mine - other + n, n)
        return jnp.where(
            ahead == 0, 0, jnp.where(ahead <= half, 2 * ahead - 1, 2 * (n - ahead))
        )

    ops["ta"] = lambda tie: turn_acts(
        tie(where), [get(x) for x in pieces], content, get("spread")[0], place_of, half, m
    )
    turned = {"tg1": names[:-3], "tg2": names[-3:-1]}
    for name, of in turned.items():
        ops[name] = lambda tie, name=name, of=of: turn_grads(
            name, [tie(get(of[0]))] + [get(x) for x in of[1:]], get("spread")[1]
        )
    late = get(names[-1])
    total = ()
    for name, lo in (("d", first), ("u", 0)):
        last = [late, get(name)]
        total = (multiply(lo, last, get("spread")[1], [get(x) for x in turned], get("ta"), total),)
    return total[0]


def solution(mesh):
    placed = (
        P(None, "tok", None),
        P(None, "tok", "out"),
        P("tok", None, None),
        P("out", None, None),
    )
    return jax.shard_map(
        shards, mesh=mesh, in_specs=placed, out_specs=P("out", "tok"), check_vma=False
    )
```

```python
import functools

import jax
import jax.numpy as jnp
from jax import lax
from jax.experimental import pallas as pl
from jax.experimental.pallas import tpu as pltpu
from jax.sharding import PartitionSpec as P

BF, F32 = jnp.bfloat16, jnp.float32
COSTS = {'tg1': 10000000000, 'tg2': 10000000000, 'turn_acts': 2000000000}


def cost(name):
    flops = COSTS.get(name)
    return flops and pl.CostEstimate(flops=flops, bytes_accessed=0, transcendentals=0)

SCALARS = pl.BlockSpec(memory_space=pltpu.SMEM)
VECTORS = pl.BlockSpec(memory_space=pltpu.VMEM)


def dot(a, b, contract):
    return lax.dot_general(a, b, (contract, ((), ())), preferred_element_type=F32)


def split(value):
    high = value.astype(BF)
    return high, (value - high.astype(F32)).astype(BF)


def run_all(copies):
    for copy in copies:
        copy.start()
    for copy in copies:
        copy.wait()


def limit(*specs):
    total = sum(2 * s.size * jnp.dtype(s.dtype).itemsize for s in specs)
    return total + 8 * 2**20


def spread_one(transposed, basis_ref, high_ref, low_ref):
    groups, span, _ = high_ref.shape
    blocks = basis_ref.shape[1]
    parts = split(basis_ref[...])
    iota = lambda shape, dim: lax.broadcasted_iota(jnp.int32, shape, dim)
    pq_row, pq_col = (
        (iota((span, 64), 1) % 8, iota((64, span), 0) // 8)
        if transposed
        else (iota((span, 64), 1) // 8, iota((64, span), 0) % 8)
    )
    keep = pq_row == iota((span, 64), 0) % 8
    repeat = (pq_col == iota((64, span), 1) % 8).astype(BF)
    diagonal = iota((span, span), 0) // 8 == iota((span, span), 1) // 8
    for g in range(groups):
        pick = iota((span, blocks), 0) // 8 + g * (span // 8) == iota((span, blocks), 1)
        pick = pick.astype(BF)
        for part, out_ref in zip(parts, (high_ref, low_ref)):
            rows = dot(pick, part, ((1,), (1,)))
            rows = jnp.where(keep, rows, 0.0).astype(BF)
            full = dot(rows, repeat, ((1,), (0,)))
            out_ref[g] = jnp.where(diagonal, full, 0.0).astype(BF)


def spread_kernel(a_ref, g_ref, a_high, a_low, g_high, g_low):
    spread_one(False, a_ref, a_high, a_low)
    spread_one(True, g_ref, g_high, g_low)


def spread(*flat):
    shapes = []
    for basis in flat:
        blocks = basis.shape[1]
        span = min(256, blocks * 8)
        shapes += [jax.ShapeDtypeStruct((blocks * 8 // span, span, span), BF)] * 2
    out = pl.pallas_call(
        spread_kernel,
        out_shape=tuple(shapes),
        compiler_params=pltpu.CompilerParams(vmem_limit_bytes=limit(*shapes)),
        cost_estimate=cost("spread"),
        name="spread",
    )(*flat)
    return out[:2], out[2:]


def cut_kernel(where_ref, acts_ref, stay_ref, go_ref, sems):
    half, _, quarter, width = stay_ref.shape
    q, z, y = where_ref[0], where_ref[1], where_ref[2]
    rows = pl.ds(pl.multiple_of(q * quarter, quarter), quarter)
    copies = []
    for k in range(half):
        for other, out_ref in enumerate((stay_ref, go_ref)):
            column = pl.multiple_of((lax.rem(z + k, half) * 2 + (y ^ other)) * width, width)
            copies.append(
                pltpu.make_async_copy(
                    acts_ref.at[:, rows, pl.ds(column, width)],
                    out_ref.at[k],
                    sems.at[2 * k + other],
                )
            )
    run_all(copies)


def cut(acts, where, n, m):
    seqs, rows, total = acts.shape
    shape = jax.ShapeDtypeStruct((n // 2, seqs, rows // m, total // n), BF)
    return pl.pallas_call(
        cut_kernel,
        in_specs=[SCALARS, pl.BlockSpec(memory_space=pltpu.HBM)],
        out_specs=[VECTORS] * 2,
        out_shape=[shape] * 2,
        scratch_shapes=[pltpu.SemaphoreType.DMA((n,))],
        compiler_params=pltpu.CompilerParams(vmem_limit_bytes=limit(shape, shape)),
        cost_estimate=cost("cut"),
        name="cut",
    )(where, pltpu.with_memory_space_constraint(acts, pltpu.HBM))


def pair_kernel(stay, came, *outs):
    for k, out in enumerate(outs):
        out[0], out[1] = stay[k], came[k]


def pair(stay, came):
    half = stay.shape[0]
    shape = jax.ShapeDtypeStruct((2, *stay.shape[1:]), BF)
    return pl.pallas_call(
        pair_kernel,
        in_specs=[VECTORS] * 2,
        out_specs=[VECTORS] * half,
        out_shape=[shape] * half,
        compiler_params=pltpu.CompilerParams(vmem_limit_bytes=limit(*[shape] * half)),
        cost_estimate=cost("pair"),
        name="pair",
    )(stay, came)


def join_kernel(*refs):
    *pieces, out = refs
    begin = 0
    for piece in pieces:
        out[begin : begin + piece.shape[0]] = piece[...]
        begin += piece.shape[0]


def join(pieces):
    count = sum(p.shape[0] for p in pieces)
    shape = jax.ShapeDtypeStruct((count, *pieces[0].shape[1:]), BF)
    return pl.pallas_call(
        join_kernel,
        in_specs=[VECTORS] * len(pieces),
        out_specs=VECTORS,
        out_shape=shape,
        compiler_params=pltpu.CompilerParams(vmem_limit_bytes=limit(shape, shape)),
        cost_estimate=cost("join"),
        name="join",
    )(*pieces)


def turn_acts_kernel(place_of, half, m, content, where_ref, *refs):
    *pieces, high, low, out_ref = refs
    groups, span, _ = high.shape
    q, z, y = where_ref[0], where_ref[1], where_ref[2]
    seqs, quarter, width = pieces[0].shape[1:]
    start_of = {}
    for piece, blocks in zip(pieces, content):
        for j, k, other in blocks:
            if (k, other) not in start_of:
                place = place_of(z, y, lax.rem(z - k + half, half), y ^ other)
                start_of[k, other] = place * m
        for g in range(groups):
            columns = pl.ds(g * span, span)
            block = piece[:, :, :, columns].reshape(len(blocks) * seqs * quarter, span)
            turned = dot(block, high[g], ((1,), (0,))) + dot(block, low[g], ((1,), (0,)))
            turned = turned.astype(BF).reshape(len(blocks), seqs, quarter, span)
            for i, (j, k, other) in enumerate(blocks):
                start = pl.multiple_of((start_of[k, other] + (q ^ j)) * quarter, quarter)
                out_ref[:, pl.ds(start, quarter), columns] = turned[i]


def turn_acts(where, pieces, content, parts, place_of, half, m):
    seqs, quarter, width = pieces[0].shape[1:]
    shape = jax.ShapeDtypeStruct((seqs, 2 * half * m * quarter, width), BF)
    return pl.pallas_call(
        functools.partial(turn_acts_kernel, place_of, half, m, content),
        in_specs=[SCALARS] + [VECTORS] * (len(pieces) + 2),
        out_specs=VECTORS,
        out_shape=shape,
        compiler_params=pltpu.CompilerParams(vmem_limit_bytes=limit(shape, shape)),
        cost_estimate=cost("turn_acts"),
        name="turn_acts",
    )(where, *pieces, *parts)


def turn_pair(high, low, first, second):
    block = jnp.concatenate([first, second], 0)
    return (dot(high, block, ((1,), (1,))) + dot(low, block, ((1,), (1,)))).astype(BF)


def turn_grads_kernel(*refs):
    *pieces, high, low, out_ref = refs
    seqs, rows, width = pieces[0].shape
    groups, span, _ = high.shape
    for g in range(groups):
        columns = pl.ds(g * span, span)
        for s in range(seqs):
            for k in range(len(pieces) // 2):
                out_ref[s, columns, pl.ds(k * 2 * rows, 2 * rows)] = turn_pair(
                    high[g], low[g], pieces[2 * k][s, :, columns], pieces[2 * k + 1][s, :, columns]
                )


def turn_grads(name, pieces, parts):
    seqs, rows, width = pieces[0].shape
    shape = jax.ShapeDtypeStruct((seqs, width, len(pieces) * rows), BF)
    return pl.pallas_call(
        turn_grads_kernel,
        in_specs=[VECTORS] * (len(pieces) + 2),
        out_specs=VECTORS,
        out_shape=shape,
        compiler_params=pltpu.CompilerParams(vmem_limit_bytes=limit(shape, shape)),
        cost_estimate=cost(name),
        name="turn_grads",
    )(*pieces, *parts)


def multiply_kernel(scale, begin, count, first, second, high, low, acts, *refs):
    grads, before, out_ref = refs[:count], refs[count:-1], refs[-1]
    step = pl.program_id(0)
    tile, width = high.shape[1], acts.shape[2]
    rows = pl.ds(pl.multiple_of(step * tile, tile), tile)
    to = rows if out_ref.shape[0] > tile else slice(None)
    turned = []
    for i in range(second.shape[0]):
        s = begin + i
        late = turn_pair(high[step], low[step], first[s, :, rows], second[i, :, rows])
        turned.append(jnp.concatenate([*(g[s, rows, :] for g in grads), late], 1))
    block = min(512, width)
    for c in range(0, width, block):
        columns = pl.ds(c, block)
        total = None
        for i, left in enumerate(turned):
            corr = dot(left, acts[begin + i, :, columns], ((1,), (0,)))
            total = corr * corr if total is None else total + corr * corr
        total = total * scale
        if before:
            total = total + before[0][rows, columns]
        out_ref[to, columns] = total


def multiply(begin, last, parts, grads, acts, before=()):
    outs = last[1].shape[2]
    _, length, width = acts.shape
    tile = parts[0].shape[1]
    shape = jax.ShapeDtypeStruct((outs, width), F32)
    strip = pl.BlockSpec((tile, width), lambda i: (i, 0))
    return pl.pallas_call(
        functools.partial(multiply_kernel, 1.0 / length, begin, len(grads)),
        grid=(outs // tile,),
        in_specs=[VECTORS] * (5 + len(grads) + len(before)),
        out_specs=strip if before else VECTORS,
        out_shape=shape,
        compiler_params=pltpu.CompilerParams(vmem_limit_bytes=limit(shape, shape)),
        cost_estimate=cost("multiply"),
        name="multiply",
    )(*last, *parts, acts, *grads, *before)


def after(value, *earlier):
    return lax.optimization_barrier((value, *earlier))[0]


TIES = {'az1': ('u1', 'd1'), 'az3': ('d1',), 'az2': ('d2',), 'x22': ('u2',), 'u': ('d1',), 'x11': ('u2',), 'x21': ('az1',)}


def shards(acts, grads, act_basis, grad_basis):
    n, m = lax.axis_size("tok"), lax.axis_size("out")
    half, seqs = n // 2, acts.shape[0]
    t, q = lax.axis_index("tok"), lax.axis_index("out")
    where = jnp.stack([q, t // 2, t % 2]).astype(jnp.int32)
    ops, done = {}, {}

    def get(name):
        if name not in done:
            earlier = [get(e) for e in TIES.get(name, ()) if e in ops]
            done[name] = ops[name](lambda v: after(v, *earlier) if earlier else v)
        return done[name]

    def send(name, source, axis, perm):
        def run(tie):
            value = tie(source())
            with jax.named_scope(name):
                return lax.ppermute(value, axis, perm)

        ops[name] = run

    def over_y(name, source):
        send(name, source, "tok", [(i, i ^ 1) for i in range(n)])

    def over_z(name, source, shift):
        send(name, source, "tok", [(i, (i // 2 + shift) % half * 2 + i % 2) for i in range(n)])

    def over_out(name, source, bit):
        send(name, source, "out", [(i, i ^ bit) for i in range(m)])

    flat = [jnp.transpose(b, (1, 2, 0)).reshape(64, -1) for b in (act_basis, grad_basis)]
    ops["spread"] = lambda tie: spread(tie(flat[0]), flat[1])
    ops["cut"] = lambda tie: cut(tie(acts), where, n, m)

    over_y("ay", lambda: get("cut")[1])
    ops["pair"] = lambda tie: pair(get("cut")[0], get("ay"))
    for k in range(1, half):
        over_z(f"az{k}", lambda k=k: get("pair")[k], k)
    come = lambda k: get(f"az{k}") if k else get("pair")[0]
    pieces, content = [], []
    middle = half // 2
    for g, ks in enumerate(([0], [k for k in range(1, half) if k != middle], [middle])):
        held = f"g{g}"
        blocks = [(0, k, other) for k in ks for other in range(2)]
        ops[held] = lambda tie, ks=ks: join([come(k) for k in ks]) if len(ks) > 1 else come(ks[0])
        bit = m // 2
        while bit:
            got = f"x{g}{bit}"
            over_out(got, lambda held=held: get(held), bit)
            theirs = [(j ^ bit, k, other) for j, k, other in blocks]
            bit //= 2
            if not bit:
                pieces.append(got)
                content.append(theirs)
                break
            both = f"{held}+"
            ops[both] = lambda tie, held=held, got=got: join([get(held), get(got)])
            held, blocks = both, blocks + theirs
        pieces.append(held)
        content.append(blocks)

    ring = [2 * z for z in range(half)] + [2 * z + 1 for z in reversed(range(half))]

    def round_ring(name, source, step):
        perm = [(ring[i], ring[(i + step) % n]) for i in range(n)]
        send(name, source, "tok", sorted(perm))

    first = seqs - 1
    ops["u0"] = ops["d0"] = lambda tie: grads
    for i in range(1, half):
        for way, step in (("u", 1), ("d", -1)):
            round_ring(f"{way}{i}", lambda way=way, i=i: get(f"{way}{i - 1}"), step)
    round_ring("u", lambda: get(f"u{half - 1}")[:first], 1)
    round_ring("d", lambda: get(f"d{half - 1}")[first:], -1)

    names = ["u0"] + [f"{way}{i}" for i in range(1, half) for way in "ud"]

    def place_of(z, y, from_z, from_y):
        mine = jnp.where(y == 0, z, n - 1 - z)
        other = jnp.where(from_y == 0, from_z, n - 1 - from_z)
        ahead = lax.rem(mine - other + n, n)
        return jnp.where(
            ahead == 0, 0, jnp.where(ahead <= half, 2 * ahead - 1, 2 * (n - ahead))
        )

    ops["ta"] = lambda tie: turn_acts(
        tie(where), [get(x) for x in pieces], content, get("spread")[0], place_of, half, m
    )
    turned = {"tg1": names[:-3], "tg2": names[-3:-1]}
    for name, of in turned.items():
        ops[name] = lambda tie, name=name, of=of: turn_grads(
            name, [tie(get(of[0]))] + [get(x) for x in of[1:]], get("spread")[1]
        )
    late = get(names[-1])
    total = ()
    for name, lo in (("d", first), ("u", 0)):
        last = [late, get(name)]
        total = (multiply(lo, last, get("spread")[1], [get(x) for x in turned], get("ta"), total),)
    return total[0]


def solution(mesh):
    placed = (
        P(None, "tok", None),
        P(None, "tok", "out"),
        P("tok", None, None),
        P("out", None, None),
    )
    return jax.shard_map(
        shards, mesh=mesh, in_specs=placed, out_specs=P("out", "tok"), check_vma=False
    )
```

```python
import functools

import jax
import jax.numpy as jnp
from jax import lax
from jax.experimental import pallas as pl
from jax.experimental.pallas import tpu as pltpu
from jax.sharding import PartitionSpec as P

BF, F32 = jnp.bfloat16, jnp.float32
COSTS = {'tg1': 10000000000, 'tg2': 10000000000, 'turn_acts': 2000000000, 'spread': 2000000000}


def cost(name):
    flops = COSTS.get(name)
    return flops and pl.CostEstimate(flops=flops, bytes_accessed=0, transcendentals=0)

SCALARS = pl.BlockSpec(memory_space=pltpu.SMEM)
VECTORS = pl.BlockSpec(memory_space=pltpu.VMEM)


def dot(a, b, contract):
    return lax.dot_general(a, b, (contract, ((), ())), preferred_element_type=F32)


def split(value):
    high = value.astype(BF)
    return high, (value - high.astype(F32)).astype(BF)


def run_all(copies):
    for copy in copies:
        copy.start()
    for copy in copies:
        copy.wait()


def limit(*specs):
    total = sum(2 * s.size * jnp.dtype(s.dtype).itemsize for s in specs)
    return total + 8 * 2**20


def spread_one(transposed, basis_ref, high_ref, low_ref):
    groups, span, _ = high_ref.shape
    blocks = basis_ref.shape[1]
    parts = split(basis_ref[...])
    iota = lambda shape, dim: lax.broadcasted_iota(jnp.int32, shape, dim)
    pq_row, pq_col = (
        (iota((span, 64), 1) % 8, iota((64, span), 0) // 8)
        if transposed
        else (iota((span, 64), 1) // 8, iota((64, span), 0) % 8)
    )
    keep = pq_row == iota((span, 64), 0) % 8
    repeat = (pq_col == iota((64, span), 1) % 8).astype(BF)
    diagonal = iota((span, span), 0) // 8 == iota((span, span), 1) // 8
    for g in range(groups):
        pick = iota((span, blocks), 0) // 8 + g * (span // 8) == iota((span, blocks), 1)
        pick = pick.astype(BF)
        for part, out_ref in zip(parts, (high_ref, low_ref)):
            rows = dot(pick, part, ((1,), (1,)))
            rows = jnp.where(keep, rows, 0.0).astype(BF)
            full = dot(rows, repeat, ((1,), (0,)))
            out_ref[g] = jnp.where(diagonal, full, 0.0).astype(BF)


def spread_kernel(a_ref, g_ref, a_high, a_low, g_high, g_low):
    spread_one(False, a_ref, a_high, a_low)
    spread_one(True, g_ref, g_high, g_low)


def spread(*flat):
    shapes = []
    for basis in flat:
        blocks = basis.shape[1]
        span = min(256, blocks * 8)
        shapes += [jax.ShapeDtypeStruct((blocks * 8 // span, span, span), BF)] * 2
    out = pl.pallas_call(
        spread_kernel,
        out_shape=tuple(shapes),
        compiler_params=pltpu.CompilerParams(vmem_limit_bytes=limit(*shapes)),
        cost_estimate=cost("spread"),
        name="spread",
    )(*flat)
    return out[:2], out[2:]


def cut_kernel(where_ref, acts_ref, stay_ref, go_ref, sems):
    half, _, quarter, width = stay_ref.shape
    q, z, y = where_ref[0], where_ref[1], where_ref[2]
    rows = pl.ds(pl.multiple_of(q * quarter, quarter), quarter)
    copies = []
    for k in range(half):
        for other, out_ref in enumerate((stay_ref, go_ref)):
            column = pl.multiple_of((lax.rem(z + k, half) * 2 + (y ^ other)) * width, width)
            copies.append(
                pltpu.make_async_copy(
                    acts_ref.at[:, rows, pl.ds(column, width)],
                    out_ref.at[k],
                    sems.at[2 * k + other],
                )
            )
    run_all(copies)


def cut(acts, where, n, m):
    seqs, rows, total = acts.shape
    shape = jax.ShapeDtypeStruct((n // 2, seqs, rows // m, total // n), BF)
    return pl.pallas_call(
        cut_kernel,
        in_specs=[SCALARS, pl.BlockSpec(memory_space=pltpu.HBM)],
        out_specs=[VECTORS] * 2,
        out_shape=[shape] * 2,
        scratch_shapes=[pltpu.SemaphoreType.DMA((n,))],
        compiler_params=pltpu.CompilerParams(vmem_limit_bytes=limit(shape, shape)),
        cost_estimate=cost("cut"),
        name="cut",
    )(where, pltpu.with_memory_space_constraint(acts, pltpu.HBM))


def pair_kernel(stay, came, *outs):
    for k, out in enumerate(outs):
        out[0], out[1] = stay[k], came[k]


def pair(stay, came):
    half = stay.shape[0]
    shape = jax.ShapeDtypeStruct((2, *stay.shape[1:]), BF)
    return pl.pallas_call(
        pair_kernel,
        in_specs=[VECTORS] * 2,
        out_specs=[VECTORS] * half,
        out_shape=[shape] * half,
        compiler_params=pltpu.CompilerParams(vmem_limit_bytes=limit(*[shape] * half)),
        cost_estimate=cost("pair"),
        name="pair",
    )(stay, came)


def join_kernel(*refs):
    *pieces, out = refs
    begin = 0
    for piece in pieces:
        out[begin : begin + piece.shape[0]] = piece[...]
        begin += piece.shape[0]


def join(pieces):
    count = sum(p.shape[0] for p in pieces)
    shape = jax.ShapeDtypeStruct((count, *pieces[0].shape[1:]), BF)
    return pl.pallas_call(
        join_kernel,
        in_specs=[VECTORS] * len(pieces),
        out_specs=VECTORS,
        out_shape=shape,
        compiler_params=pltpu.CompilerParams(vmem_limit_bytes=limit(shape, shape)),
        cost_estimate=cost("join"),
        name="join",
    )(*pieces)


def turn_acts_kernel(place_of, half, m, content, where_ref, *refs):
    *pieces, high, low, out_ref = refs
    groups, span, _ = high.shape
    q, z, y = where_ref[0], where_ref[1], where_ref[2]
    seqs, quarter, width = pieces[0].shape[1:]
    start_of = {}
    for piece, blocks in zip(pieces, content):
        for j, k, other in blocks:
            if (k, other) not in start_of:
                place = place_of(z, y, lax.rem(z - k + half, half), y ^ other)
                start_of[k, other] = place * m
        for g in range(groups):
            columns = pl.ds(g * span, span)
            block = piece[:, :, :, columns].reshape(len(blocks) * seqs * quarter, span)
            turned = dot(block, high[g], ((1,), (0,))) + dot(block, low[g], ((1,), (0,)))
            turned = turned.astype(BF).reshape(len(blocks), seqs, quarter, span)
            for i, (j, k, other) in enumerate(blocks):
                start = pl.multiple_of((start_of[k, other] + (q ^ j)) * quarter, quarter)
                out_ref[:, pl.ds(start, quarter), columns] = turned[i]


def turn_acts(where, pieces, content, parts, place_of, half, m):
    seqs, quarter, width = pieces[0].shape[1:]
    shape = jax.ShapeDtypeStruct((seqs, 2 * half * m * quarter, width), BF)
    return pl.pallas_call(
        functools.partial(turn_acts_kernel, place_of, half, m, content),
        in_specs=[SCALARS] + [VECTORS] * (len(pieces) + 2),
        out_specs=VECTORS,
        out_shape=shape,
        compiler_params=pltpu.CompilerParams(vmem_limit_bytes=limit(shape, shape)),
        cost_estimate=cost("turn_acts"),
        name="turn_acts",
    )(where, *pieces, *parts)


def turn_pair(high, low, first, second):
    block = jnp.concatenate([first, second], 0)
    return (dot(high, block, ((1,), (1,))) + dot(low, block, ((1,), (1,)))).astype(BF)


def turn_grads_kernel(*refs):
    *pieces, high, low, out_ref = refs
    seqs, rows, width = pieces[0].shape
    groups, span, _ = high.shape
    for g in range(groups):
        columns = pl.ds(g * span, span)
        for s in range(seqs):
            for k in range(len(pieces) // 2):
                out_ref[s, columns, pl.ds(k * 2 * rows, 2 * rows)] = turn_pair(
                    high[g], low[g], pieces[2 * k][s, :, columns], pieces[2 * k + 1][s, :, columns]
                )


def turn_grads(name, pieces, parts):
    seqs, rows, width = pieces[0].shape
    shape = jax.ShapeDtypeStruct((seqs, width, len(pieces) * rows), BF)
    return pl.pallas_call(
        turn_grads_kernel,
        in_specs=[VECTORS] * (len(pieces) + 2),
        out_specs=VECTORS,
        out_shape=shape,
        compiler_params=pltpu.CompilerParams(vmem_limit_bytes=limit(shape, shape)),
        cost_estimate=cost(name),
        name="turn_grads",
    )(*pieces, *parts)


def multiply_kernel(scale, begin, count, first, second, high, low, acts, *refs):
    grads, before, out_ref = refs[:count], refs[count:-1], refs[-1]
    step = pl.program_id(0)
    tile, width = high.shape[1], acts.shape[2]
    rows = pl.ds(pl.multiple_of(step * tile, tile), tile)
    to = rows if out_ref.shape[0] > tile else slice(None)
    turned = []
    for i in range(second.shape[0]):
        s = begin + i
        late = turn_pair(high[step], low[step], first[s, :, rows], second[i, :, rows])
        turned.append(jnp.concatenate([*(g[s, rows, :] for g in grads), late], 1))
    block = min(512, width)
    for c in range(0, width, block):
        columns = pl.ds(c, block)
        total = None
        for i, left in enumerate(turned):
            corr = dot(left, acts[begin + i, :, columns], ((1,), (0,)))
            total = corr * corr if total is None else total + corr * corr
        total = total * scale
        if before:
            total = total + before[0][rows, columns]
        out_ref[to, columns] = total


def multiply(begin, last, parts, grads, acts, before=()):
    outs = last[1].shape[2]
    _, length, width = acts.shape
    tile = parts[0].shape[1]
    shape = jax.ShapeDtypeStruct((outs, width), F32)
    strip = pl.BlockSpec((tile, width), lambda i: (i, 0))
    return pl.pallas_call(
        functools.partial(multiply_kernel, 1.0 / length, begin, len(grads)),
        grid=(outs // tile,),
        in_specs=[VECTORS] * (5 + len(grads) + len(before)),
        out_specs=strip if before else VECTORS,
        out_shape=shape,
        compiler_params=pltpu.CompilerParams(vmem_limit_bytes=limit(shape, shape)),
        cost_estimate=cost("multiply"),
        name="multiply",
    )(*last, *parts, acts, *grads, *before)


def after(value, *earlier):
    return lax.optimization_barrier((value, *earlier))[0]


TIES = {'az1': ('u1', 'd1'), 'az3': ('d1',), 'az2': ('d2',), 'u': ('d1',), 'x11': ('u2',), 'x21': ('az1',), 'u2': ('u1',), 'x01': ('x02',)}


def shards(acts, grads, act_basis, grad_basis):
    n, m = lax.axis_size("tok"), lax.axis_size("out")
    half, seqs = n // 2, acts.shape[0]
    t, q = lax.axis_index("tok"), lax.axis_index("out")
    where = jnp.stack([q, t // 2, t % 2]).astype(jnp.int32)
    ops, done = {}, {}

    def get(name):
        if name not in done:
            earlier = [get(e) for e in TIES.get(name, ()) if e in ops]
            done[name] = ops[name](lambda v: after(v, *earlier) if earlier else v)
        return done[name]

    def send(name, source, axis, perm):
        def run(tie):
            value = tie(source())
            with jax.named_scope(name):
                return lax.ppermute(value, axis, perm)

        ops[name] = run

    def over_y(name, source):
        send(name, source, "tok", [(i, i ^ 1) for i in range(n)])

    def over_z(name, source, shift):
        send(name, source, "tok", [(i, (i // 2 + shift) % half * 2 + i % 2) for i in range(n)])

    def over_out(name, source, bit):
        send(name, source, "out", [(i, i ^ bit) for i in range(m)])

    flat = [jnp.transpose(b, (1, 2, 0)).reshape(64, -1) for b in (act_basis, grad_basis)]
    ops["spread"] = lambda tie: spread(tie(flat[0]), flat[1])
    ops["cut"] = lambda tie: cut(tie(acts), where, n, m)

    over_y("ay", lambda: get("cut")[1])
    ops["pair"] = lambda tie: pair(get("cut")[0], get("ay"))
    for k in range(1, half):
        over_z(f"az{k}", lambda k=k: get("pair")[k], k)
    come = lambda k: get(f"az{k}") if k else get("pair")[0]
    pieces, content = [], []
    middle = half // 2
    for g, ks in enumerate(([0], [k for k in range(1, half) if k != middle], [middle])):
        held = f"g{g}"
        blocks = [(0, k, other) for k in ks for other in range(2)]
        ops[held] = lambda tie, ks=ks: join([come(k) for k in ks]) if len(ks) > 1 else come(ks[0])
        bit = m // 2
        while bit:
            got = f"x{g}{bit}"
            over_out(got, lambda held=held: get(held), bit)
            theirs = [(j ^ bit, k, other) for j, k, other in blocks]
            bit //= 2
            if not bit:
                pieces.append(got)
                content.append(theirs)
                break
            both = f"{held}+"
            ops[both] = lambda tie, held=held, got=got: join([get(held), get(got)])
            held, blocks = both, blocks + theirs
        pieces.append(held)
        content.append(blocks)

    ring = [2 * z for z in range(half)] + [2 * z + 1 for z in reversed(range(half))]

    def round_ring(name, source, step):
        perm = [(ring[i], ring[(i + step) % n]) for i in range(n)]
        send(name, source, "tok", sorted(perm))

    first = seqs - 1
    ops["u0"] = ops["d0"] = lambda tie: grads
    for i in range(1, half):
        for way, step in (("u", 1), ("d", -1)):
            round_ring(f"{way}{i}", lambda way=way, i=i: get(f"{way}{i - 1}"), step)
    round_ring("u", lambda: get(f"u{half - 1}")[:first], 1)
    round_ring("d", lambda: get(f"d{half - 1}")[first:], -1)

    names = ["u0"] + [f"{way}{i}" for i in range(1, half) for way in "ud"]

    def place_of(z, y, from_z, from_y):
        mine = jnp.where(y == 0, z, n - 1 - z)
        other = jnp.where(from_y == 0, from_z, n - 1 - from_z)
        ahead = lax.rem(mine - other + n, n)
        return jnp.where(
            ahead == 0, 0, jnp.where(ahead <= half, 2 * ahead - 1, 2 * (n - ahead))
        )

    ops["ta"] = lambda tie: turn_acts(
        tie(where), [get(x) for x in pieces], content, get("spread")[0], place_of, half, m
    )
    turned = {"tg1": names[:-3], "tg2": names[-3:-1]}
    for name, of in turned.items():
        ops[name] = lambda tie, name=name, of=of: turn_grads(
            name, [tie(get(of[0]))] + [get(x) for x in of[1:]], get("spread")[1]
        )
    late = get(names[-1])
    total = ()
    for name, lo in (("d", first), ("u", 0)):
        last = [late, get(name)]
        total = (multiply(lo, last, get("spread")[1], [get(x) for x in turned], get("ta"), total),)
    return total[0]


def solution(mesh):
    placed = (
        P(None, "tok", None),
        P(None, "tok", "out"),
        P("tok", None, None),
        P("out", None, None),
    )
    return jax.shard_map(
        shards, mesh=mesh, in_specs=placed, out_specs=P("out", "tok"), check_vma=False
    )
```
